512 devices in a mesh: node: 16 (over x, y_hi, core), dp: 32 (over z, y_lo).
Axes of the slice: x: 4, y: 4 (y_hi: 2, y_lo: 2; y = y_hi * 2 + y_lo), z: 16, core: 2. Of those that a mesh axis runs over, the one named last changes fastest.
Arguments:
- tokens_in: bfloat16 [65536, 8192], P(('node', 'dp')), may hold values from -4 to 4
- gain: float32 [8192], replicated, may hold values from 0.5 to 1.5
- value_weight: bfloat16 [8192, 512], P('node'), may hold values from -1 to 1
- value_grad: bfloat16 [65536, 512], P(('node', 'dp')), may hold values from -0.24 to 0.24
Outputs:
- weight_grad: float32 [8192, 512], P(('node', 'dp'))
- gain_grad: float32 [8192], P(('node', 'dp'))
- input_grad: bfloat16 [65536, 8192], P(('node', 'dp'))
The draws below stay inside these ranges and needn't reach their ends.
All inputs are finite; a program needn't handle non-finite values.
Results may differ from the reference program's by a relative error of at most 0.035.
Values may be sent and summed in bfloat16 or wider, within the bound.
A program may use at most 64 MiB of HBM per device.

```python
import math
import jax
import jax.numpy as jnp
from jax import lax

D = 8192
HD = 128
KVH = 4
TOK_DEV = 128
TOKENS = 65536
N_NODE = 16
N_DP = 32


def common_parts(key):
    beta_key, zeta_key = jax.random.split(key)
    beta = jax.random.truncated_normal(beta_key, -2.0, 2.0, (TOKENS, 1), jnp.float32)
    zeta = jax.random.truncated_normal(zeta_key, -2.0, 2.0, (1, KVH * HD), jnp.float32)
    return (beta, zeta)


def draw_tokens_in(key, part):
    beta, zeta = common_parts(key)
    key = jax.random.fold_in(key, 3)
    noise_key, row_key, col_key = jax.random.split(key, 3)
    row_scale = jnp.exp(jax.random.uniform(row_key, (TOKENS, 1), jnp.float32, 0.0, math.log(10.0)))
    col_scale = jnp.exp(jax.random.uniform(col_key, (1, D), jnp.float32, 0.0, math.log(10.0)))
    base_values = jax.random.truncated_normal(noise_key, -4.0, 4.0, (TOKENS, D), jnp.float32)
    pattern = jnp.tile(zeta, (1, D // (KVH * HD)))
    return (0.005 * (base_values + beta * pattern) * row_scale * col_scale).astype(jnp.bfloat16)


def draw_value_weight(key, part):
    key = jax.random.fold_in(key, 5)
    out_cols = KVH * HD
    noise = jax.random.truncated_normal(key, -4.0, 4.0, (D, out_cols), jnp.float32) * (1.0 / math.sqrt(D))
    row_ids = jax.lax.broadcasted_iota(jnp.int32, (D, out_cols), 0)
    col_ids = jax.lax.broadcasted_iota(jnp.int32, (D, out_cols), 1)
    matched = (row_ids % out_cols == col_ids).astype(jnp.float32)
    return (noise + math.sqrt(out_cols / D) * matched).astype(jnp.bfloat16)


def draw_value_grad(key, part):
    beta, zeta = common_parts(key)
    key = jax.random.fold_in(key, 9)
    noise_key, sign_key = jax.random.split(key)
    noise = jax.random.truncated_normal(noise_key, -4.0, 4.0, (TOKENS, KVH * HD), jnp.float32)
    signs = 2.0 * jax.random.bernoulli(sign_key, 0.5, (TOKENS, 1)).astype(jnp.float32) - 1.0
    return (0.03 * (noise + signs * beta * zeta)).astype(jnp.bfloat16)


def setup_inputs(seed: int = 0) -> dict:
    key_of = jax.random.split(jax.random.key(seed), 5)
    return {
        "tokens_in": draw_tokens_in(jax.random.fold_in(key_of[4], 71), 0),
        "gain": jnp.clip(1.0 + 0.1 * jax.random.normal(key_of[1], (D,), jnp.float32), 0.5, 1.5),
        "value_weight": draw_value_weight(jax.random.fold_in(key_of[4], 71), 0),
        "value_grad": draw_value_grad(jax.random.fold_in(key_of[4], 71), 0),
    }


EPS = 1e-05

def normalize(tokens_in, gain):
    tokens_f32 = tokens_in.astype(jnp.float32)
    inv_rms = lax.rsqrt(lax.optimization_barrier(jnp.mean(tokens_f32 * tokens_f32, axis=1, keepdims=True)) + EPS)
    unit = tokens_f32 * inv_rms
    normed = unit.astype(jnp.bfloat16)
    scaled = (normed.astype(jnp.float32) * gain.astype(jnp.float32)).astype(jnp.bfloat16)
    return (inv_rms, unit, normed, scaled)

def input_gradient(normed_grad, gain, inv_rms, unit):
    feature_grad = normed_grad * gain.astype(jnp.float32)
    spread = lax.optimization_barrier(jnp.mean(feature_grad * unit, axis=1, keepdims=True))
    return (inv_rms * (feature_grad - unit * spread)).astype(jnp.bfloat16)

def reference(tokens_in, gain, value_weight, value_grad):
    out_cols = KVH * HD
    weight_f32 = value_weight.astype(jnp.float32)

    def group_terms(group_index):
        first_tok = group_index * TOK_DEV
        tok_slice = lax.dynamic_slice_in_dim(tokens_in, first_tok, TOK_DEV, 0)
        grad_slice = lax.dynamic_slice_in_dim(value_grad, first_tok, TOK_DEV, 0)
        inv_rms, unit, normed, scaled = normalize(tok_slice, gain)
        grad_f32 = grad_slice.astype(jnp.float32)
        normed_grad = jnp.dot(grad_f32, weight_f32.T, precision=lax.Precision.HIGHEST)
        gain_term = lax.optimization_barrier(jnp.sum(normed.astype(jnp.float32) * normed_grad, axis=0)).astype(jnp.bfloat16)
        weight_term = jnp.dot(scaled.astype(jnp.float32).T, grad_f32, precision=lax.Precision.HIGHEST).astype(jnp.bfloat16)
        input_grad = input_gradient(normed_grad, gain, inv_rms, unit)
        return (weight_term, gain_term, input_grad)

    def outer(totals, data_index):

        def inner(running, node_index):
            weight_term, gain_term, input_grad = group_terms(node_index * N_DP + data_index)
            weight_term = lax.optimization_barrier(weight_term)
            gain_term = lax.optimization_barrier(gain_term)
            return ((running[0] + weight_term.astype(jnp.float32), running[1] + gain_term.astype(jnp.float32)), input_grad)
        start_sums = (jnp.zeros((D, out_cols), jnp.float32), jnp.zeros((D,), jnp.float32))
        (weight_sum, gain_sum), grads_in = lax.scan(inner, start_sums, jnp.arange(N_NODE, dtype=jnp.int32))
        weight_group = lax.optimization_barrier(weight_sum.astype(jnp.bfloat16))
        gain_group = lax.optimization_barrier(gain_sum.astype(jnp.bfloat16))
        return ((totals[0] + weight_group.astype(jnp.float32), totals[1] + gain_group.astype(jnp.float32)), grads_in)
    start_totals = (jnp.zeros((D, out_cols), jnp.float32), jnp.zeros((D,), jnp.float32))
    (weight_grad, gain_grad), stacked = lax.scan(outer, start_totals, jnp.arange(N_DP, dtype=jnp.int32))
    input_grad = jnp.transpose(stacked, (1, 0, 2, 3)).reshape(TOKENS, D)
    return (weight_grad, gain_grad, input_grad)
```

```python
import jax
import jax.numpy as jnp
from jax import lax
from jax.experimental import pallas as pl
from jax.experimental.pallas import tpu as pltpu
from jax.sharding import PartitionSpec as P

D = 8192
EPS = 1e-05
NX, NY, NZ = 4, 4, 16
T = 128
K = 512
F = 256
BF, F32 = jnp.bfloat16, jnp.float32
MESH = pl.DeviceIdType.MESH


def device_at(x, y, z, core):
    return (x * 4 + (y // 2) * 2 + core, z * 2 + y % 2)


def kernel(
    tok_hbm, gain_ref, weight_hbm, vg_hbm,
    wg_ref, gg_ref, ig_hbm,
    tok, shard, vgall, inv, nsend, nall, wall, ngs, ngr,
    s1, s2, r1, r2, t1, t2, u1, u2, vb, zr, outb,
    load_sem, vg_s, vg_r, tok_s, tok_r, ax_s, ax_r, ay_s, ay_r, ap_s, ap_r,
    back_s, back_r, p1_s, p1_r, p2_s, p2_r, q1_s, q1_r, q2_s, q2_r, z_s, z_r, out_sem,
):
    node, dp = lax.axis_index("node"), lax.axis_index("dp")
    x, yh, c = node // 4, (node // 2) % 2, node % 2
    z, yl = dp // 2, dp % 2
    y = yh * 2 + yl
    p = z % 2
    zs = (z + 17 - 2 * c) % NZ
    zup, zdn = (z + 1) % NZ, (z + 15) % NZ
    me = lambda **kw: device_at(kw.get("x", x), kw.get("y", y), kw.get("z", z), kw.get("c", c))

    def send(src, dst, ssem, rsem, to):
        return pltpu.make_async_remote_copy(
            src_ref=src, dst_ref=dst, send_sem=ssem, recv_sem=rsem, device_id=to, device_id_type=MESH
        )

    load_tok = pltpu.make_async_copy(tok_hbm, tok, load_sem.at[0])
    load_w = pltpu.make_async_copy(weight_hbm, shard, load_sem.at[1])
    load_vg = pltpu.make_async_copy(vg_hbm, vgall.at[pl.ds(0, T)], load_sem.at[2])
    load_tok.start()
    load_w.start()
    load_vg.start()

    barrier = pltpu.get_barrier_semaphore()
    partners = [me(x=(x + d) % NX) for d in (1, 2, 3)] + [me(y=(y + d) % NY) for d in (1, 2, 3)]
    partners += [me(c=1 - c), me(z=zup, c=1 - c), me(z=zdn, c=1 - c)]
    for to in partners:
        pl.semaphore_signal(barrier, inc=1, device_id=to, device_id_type=MESH)

    def greet(d, carry):
        pl.semaphore_signal(barrier, inc=1, device_id=me(z=(z + d) % NZ), device_id_type=MESH)
        return carry

    lax.fori_loop(1, NZ, greet, 0)

    load_tok.wait()

    def squares(i, acc):
        t = tok[:, pl.ds(pl.multiple_of(i * K, K), K)].astype(F32)
        t = t * t
        return acc + ((t[:, 0:128] + t[:, 128:256]) + (t[:, 256:384] + t[:, 384:512]))

    acc = lax.fori_loop(0, D // K, squares, jnp.zeros((T, 128), F32))
    mean = jnp.sum(acc, axis=1, keepdims=True) * (1.0 / D)
    inv[...] = jnp.broadcast_to(lax.rsqrt(mean + EPS), (T, 128))

    def column(j, xt, ht):
        cc = c if j in (0, 2) else 1 - c
        pp = p if j < 2 else 1 - p
        return pl.multiple_of(xt * 2048 + ht * 1024 + cc * 512 + pp * 256, 256)

    def unit_tile(j, xt, ht):
        scale = inv[...]
        scale = jnp.concatenate([scale, scale], axis=1)
        return tok[:, pl.ds(column(j, xt, ht), F)].astype(F32) * scale

    load_w.wait()
    load_vg.wait()
    pl.semaphore_wait(barrier, len(partners) + NZ - 1)

    slot = 3 - c
    helpers = [(me(c=1 - c), 1), (me(z=zs), slot), (me(z=zs, c=1 - c), slot)]
    vg_copies = [
        send(vgall.at[pl.ds(0, T)], vgall.at[pl.ds(sl * T, T)], vg_s.at[i], vg_r.at[sl - 1], to)
        for i, (to, sl) in enumerate(helpers)
    ]
    for copy in vg_copies:
        copy.start()

    own_rows = pl.ds(pl.multiple_of(p * F, F), F)
    half = 1 - yl
    ax = [send(shard.at[own_rows], wall.at[x, yh], ax_s.at[d - 1], ax_r.at[d - 1], me(x=(x + d) % NX)) for d in (1, 2, 3)]
    out_half = pl.ds(pl.multiple_of(half * 128, 128), 128)
    in_half = pl.ds(pl.multiple_of(yl * 128, 128), 128)
    ay = [
        send(
            shard.at[pl.ds(pl.multiple_of(p * F + half * 128, 128), 128)] if d == 0 else wall.at[(x + d) % NX, yh, out_half],
            wall.at[(x + d) % NX, yh, out_half], ay_s.at[d], ay_r.at[d], me(y=3 - y),
        )
        for d in range(NX)
    ]
    ap = [
        send(
            wall.at[(x + d) % NX, 1 - yh, in_half], wall.at[(x + d) % NX, 1 - yh, in_half],
            ap_s.at[d], ap_r.at[d], me(y=yh * 2 + 1 - yl),
        )
        for d in range(NX)
    ]
    ay_in = [
        send(
            wall.at[(x + d) % NX, 1 - yh, in_half], wall.at[(x + d) % NX, 1 - yh, in_half],
            ay_s.at[d], ay_r.at[d], me(y=3 - y),
        )
        for d in range(NX)
    ]
    ay[0].start()
    ax[0].start()
    ax[2].start()
    ax[1].start()

    def token_copy(i, xt):
        to, sl = helpers[i]
        return send(
            nsend.at[i, xt], nall.at[xt, :, pl.ds(sl * T, T)], tok_s.at[i, xt], tok_r.at[sl - 1, xt], to
        )

    def normalize(m, carry):
        xt = (x + 2 + m) % NX
        for ht in range(2):
            for j in (2, 3, 1, 0):
                tile = unit_tile(j, xt, ht).astype(BF)
                if j == 0:
                    nall[xt, ht, 0:T] = tile
                else:
                    nsend[(0, 0, 1, 2)[j], xt, ht] = tile
        for i in (1, 2, 0):
            token_copy(i, xt).start()
        return carry

    lax.fori_loop(0, NX, normalize, 0)
    wall[x, yh] = shard[own_rows]

    for sl in (1, 2, 3):
        send(vgall.at[pl.ds(0, T)], vgall.at[pl.ds(sl * T, T)], vg_s.at[0], vg_r.at[sl - 1], me(c=1 - c)).wait_recv()

    def p1_copy(d, ht):
        return send(
            s1.at[(x + d) % NX, pl.ds(ht * 2, 2)], r1.at[d - 1, pl.ds(ht * 2, 2)],
            p1_s.at[d - 1, ht], p1_r.at[d - 1, ht], me(x=(x + d) % NX),
        )

    def p2_copy(e, xt):
        return send(
            s2.at[(y + e) % NY, xt], r2.at[e - 1, xt], p2_s.at[e - 1, xt], p2_r.at[e - 1, xt], me(y=(y + e) % NY)
        )

    def weight_tile(xt, ht):
        total = lax.dot_general(nall[xt, ht], vgall[...], (((0,), (0,)), ((), ())), preferred_element_type=F32)
        total = total.astype(BF).reshape(8, 2, 16, K)
        for low in range(2):
            part = total[:, low].reshape(128, K)
            s1[xt, ht * 2 + low] = part[:, 0:256]
            s2[ht * 2 + low, xt] = part[:, 256:512]

    def weight_step(m):
        d = (2 + m) % NX
        xt = (x + d) % NX
        for sl in (1, 2, 3):
            send(nsend.at[0, xt], nall.at[xt, :, pl.ds(sl * T, T)], tok_s.at[0, xt], tok_r.at[sl - 1, xt], me(c=1 - c)).wait_recv()

        def tiles(h, carry):
            ht = (yh + 1 + h) % 2
            weight_tile(xt, ht)
            if d != 0:
                p1_copy(d, ht).start()
            for low in range(2):
                e = (ht * 2 + low - y + NY) % NY

                @pl.when(e != 0)
                def _():
                    p2_copy(e, xt).start()

            return carry

        lax.fori_loop(0, 2, tiles, 0)

    for i in (0, 2):
        ax[i].wait_recv()
    ay[3].start()
    ay[1].start()
    weight_step(0)
    ay_in[0].wait_recv()
    ap[0].start()
    ax[1].wait_recv()
    ay[2].start()
    weight_step(1)
    for d in (1, 3):
        ay_in[d].wait_recv()
        ap[d].start()
    weight_step(2)
    weight_step(3)
    ay_in[2].wait_recv()
    ap[2].start()

    owners = [(me(c=1 - c), 1), (me(z=zup, c=1), 3 - c), (me(z=zdn, c=0), 2 + c)]

    def back_copy(i, xt):
        to, j = owners[i]
        return send(ngs.at[xt, :, pl.ds(i * T, T)], ngr.at[j, xt], back_s.at[i, xt], back_r.at[j - 1, xt], to)

    def grad_tiles(xt):
        def tiles(ht, carry):
            ng = lax.dot_general(
                vgall[...], wall[xt, ht], (((1,), (1,)), ((), ())), preferred_element_type=F32
            ).astype(BF)
            ngr[0, xt, ht] = ng[0:T]
            ngs[xt, ht] = ng[T:]
            return carry

        lax.fori_loop(0, 2, tiles, 0)
        for i in (1, 2, 0):
            back_copy(i, xt).start()

    for d in (0, 1, 3, 2):
        send(
            wall.at[(x + d) % NX, 1 - yh, out_half], wall.at[(x + d) % NX, 1 - yh, out_half],
            ap_s.at[d], ap_r.at[d], me(y=yh * 2 + 1 - yl),
        ).wait_recv()
        grad_tiles((x + d) % NX)

    def q1_copy(e):
        return send(t1.at[(y + e) % NY], u1.at[e - 1], q1_s.at[e - 1], q1_r.at[e - 1], me(y=(y + e) % NY))

    def q2_copy(d):
        return send(t2.at[(x + d) % NX], u2.at[d - 1], q2_s.at[d - 1], q2_r.at[d - 1], me(x=(x + d) % NX))

    for ht in range(2):
        for d in (1, 2, 3):
            p1_copy(d, ht).wait_recv()

    def add1(e, carry):
        yt = (y + e) % NY
        total = s1[x, yt].astype(F32) + r1[0, yt].astype(F32) + r1[1, yt].astype(F32) + r1[2, yt].astype(F32)
        t1[yt] = total.astype(BF)

        @pl.when(e != NY)
        def _():
            q1_copy(e).start()

        return carry

    lax.fori_loop(1, NY + 1, add1, 0)
    for xt in range(NX):
        for e in (1, 2, 3):
            p2_copy(e, xt).wait_recv()

    def add2(d, carry):
        xt = (x + d) % NX
        total = s2[y, xt].astype(F32) + r2[0, xt].astype(F32) + r2[1, xt].astype(F32) + r2[2, xt].astype(F32)
        t2[xt] = total.astype(BF)

        @pl.when(d != NX)
        def _():
            q2_copy(d).start()

        return carry

    lax.fori_loop(1, NX + 1, add2, 0)

    for e in (1, 2, 3):
        q1_copy(e).wait_recv()
    total = t1[y].astype(F32) + u1[0].astype(F32) + u1[1].astype(F32) + u1[2].astype(F32)
    vb[:, :, 0:256] = total.astype(BF).reshape(8, 16, 256)
    for d in (1, 2, 3):
        q2_copy(d).wait_recv()
    total = t2[x].astype(F32) + u2[0].astype(F32) + u2[1].astype(F32) + u2[2].astype(F32)
    vb[:, :, 256:512] = total.astype(BF).reshape(8, 16, 256)

    def z_copy(k):
        return send(vb.at[k], zr.at[z // 2], z_s.at[k], z_r.at[z // 2], me(z=p * 8 + k))

    def z_start(i, carry):
        k = (z + i) % 8

        @pl.when(p * 8 + k != z)
        def _():
            z_copy(k).start()

        @pl.when(p * 8 + k == z)
        def _():
            zr[z // 2] = vb[k]

        return carry

    lax.fori_loop(0, 8, z_start, 0)

    for j in (1, 2, 3):
        for xt in range(NX):
            send(ngs.at[xt, :, pl.ds(0, T)], ngr.at[j, xt], back_s.at[0, xt], back_r.at[j - 1, xt], me(c=1 - c)).wait_recv()

    def feature_tile(j, xt, ht):
        return ngr[j, xt, ht].astype(F32) * gain_ref[:, pl.ds(column(j, xt, ht), F)]

    def spread_tile(i, acc):
        xt, ht = i // 2, i % 2
        for j in range(4):
            prod = feature_tile(j, xt, ht) * unit_tile(j, xt, ht)
            acc = acc + (prod[:, 0:128] + prod[:, 128:256])
        return acc

    acc = lax.fori_loop(0, 8, spread_tile, jnp.zeros((T, 128), F32))
    spread = jnp.sum(acc, axis=1, keepdims=True) * (1.0 / D)

    def input_tile(i, carry):
        xt, ht = i // 2, i % 2
        scale = inv[...]
        scale = jnp.concatenate([scale, scale], axis=1)
        for j in range(4):
            grad = scale * (feature_tile(j, xt, ht) - unit_tile(j, xt, ht) * spread)
            outb[:, pl.ds(column(j, xt, ht), F)] = grad.astype(BF)
        return carry

    lax.fori_loop(0, 8, input_tile, 0)
    store = pltpu.make_async_copy(outb, ig_hbm, out_sem.at[0])
    store.start()

    def z_wait(k, carry):
        @pl.when(2 * k + z // 8 != z)
        def _():
            send(vb.at[k], zr.at[k], z_s.at[k], z_r.at[k], me(z=(z + 1) % NZ)).wait_recv()

        return carry

    lax.fori_loop(0, 8, z_wait, 0)
    total = zr[0].astype(F32)
    for k in range(1, 8):
        total = total + zr[k].astype(F32)

    lanes = lax.broadcasted_iota(jnp.int32, (16, 128), 1)
    rows = lax.broadcasted_iota(jnp.int32, (16, 128), 0)
    block = gain_ref[:, pl.ds(pl.multiple_of(node * 512 + (dp // 8) * 128, 128), 128)]
    picked = jnp.where(lanes == rows + (dp % 8) * 16, jnp.broadcast_to(block, (16, 128)), 0.0)
    wg_ref[...] = total * jnp.sum(picked, axis=1, keepdims=True)
    own = shard[pl.ds(pl.multiple_of(dp * 16, 16), 16)].astype(F32)
    gain_sum = jnp.sum(own * total, axis=1, keepdims=True)
    spread_out = jnp.where(lanes == rows, jnp.broadcast_to(gain_sum, (16, 128)), 0.0)
    gg_ref[...] = jnp.sum(spread_out, axis=0, keepdims=True)

    for copy in vg_copies + ax + ay + ap:
        copy.wait_send()
    for i in range(3):
        for xt in range(NX):
            token_copy(i, xt).wait_send()
            back_copy(i, xt).wait_send()
            p2_copy(i + 1, xt).wait_send()
        for ht in range(2):
            p1_copy(i + 1, ht).wait_send()
        q1_copy(i + 1).wait_send()
        q2_copy(i + 1).wait_send()

    def z_sent(k, carry):
        @pl.when(p * 8 + k != z)
        def _():
            z_copy(k).wait_send()

        return carry

    lax.fori_loop(0, 8, z_sent, 0)
    store.wait()


def on_device(tokens_in, gain, value_weight, value_grad):
    vmem, dma = pltpu.VMEM, pltpu.SemaphoreType.DMA
    scratch = [
        vmem((T, D), BF), vmem((K, K), BF), vmem((4 * T, K), BF), vmem((T, 128), F32),
        vmem((3, NX, 2, T, F), BF), vmem((NX, 2, 4 * T, F), BF), vmem((NX, 2, F, K), BF),
        vmem((NX, 2, 3 * T, F), BF), vmem((4, NX, 2, T, F), BF),
        vmem((NX, NY, 128, 256), BF), vmem((NY, NX, 128, 256), BF),
        vmem((3, NY, 128, 256), BF), vmem((3, NX, 128, 256), BF),
        vmem((NY, 128, 256), BF), vmem((NX, 128, 256), BF),
        vmem((3, 128, 256), BF), vmem((3, 128, 256), BF),
        vmem((8, 16, K), BF), vmem((8, 16, K), BF), vmem((T, D), BF),
    ]
    sems = [(3,)] + [(3,)] * 2 + [(3, NX)] * 2 + [(3,)] * 2 + [(4,)] * 4 + [(3, NX)] * 2
    sems += [(3, 2)] * 2 + [(3, NX)] * 2 + [(3,)] * 4 + [(8,)] * 2 + [(1,)]
    any_space = pl.BlockSpec(memory_space=pl.ANY)
    in_vmem = pl.BlockSpec(memory_space=pltpu.VMEM)
    weight_grad, gain_grad, input_grad = pl.pallas_call(
        kernel,
        out_shape=(
            jax.ShapeDtypeStruct((16, K), F32),
            jax.ShapeDtypeStruct((1, 128), F32),
            jax.ShapeDtypeStruct((T, D), BF),
        ),
        in_specs=[any_space, in_vmem, any_space, any_space],
        out_specs=(in_vmem, in_vmem, any_space),
        scratch_shapes=scratch + [dma(s) for s in sems],
        compiler_params=pltpu.CompilerParams(
            collective_id=0, has_side_effects=True, vmem_limit_bytes=48 * 1024 * 1024
        ),
    )(tokens_in, gain.reshape(1, D), value_weight, value_grad)
    return weight_grad, gain_grad[0, :16], input_grad


def solution(mesh):
    placed = (P(("node", "dp"), None), P(), P("node", None), P(("node", "dp"), None))
    return jax.shard_map(
        on_device,
        mesh=mesh,
        in_specs=placed,
        out_specs=(P(("node", "dp"), None), P(("node", "dp")), P(("node", "dp"), None)),
        check_vma=False,
    )
```

```python
import jax
import jax.numpy as jnp
from jax import lax
from jax.experimental import pallas as pl
from jax.experimental.pallas import tpu as pltpu
from jax.sharding import PartitionSpec as P

D = 8192
EPS = 1e-05
NX, NY, NZ = 4, 4, 16
T = 128
K = 512
F = 256
BF, F32 = jnp.bfloat16, jnp.float32
MESH = pl.DeviceIdType.MESH


def device_at(x, y, z, core):
    return (x * 4 + (y // 2) * 2 + core, z * 2 + y % 2)


def kernel(
    tok_hbm, gain_hbm, weight_hbm, vg_hbm,
    wg_ref, gg_ref, ig_ref,
    tok, gain_ref, shard, vgall, inv, nsend, nall, wall, ngs, ngr,
    s1, s2, r1, r2, t1, t2, u1, u2, vb, zr,
    load_sem, vg_s, vg_r, tok_s, tok_r, ax_s, ax_r, ay_s, ay_r, ap_s, ap_r,
    back_s, back_r, p1_s, p1_r, p2_s, p2_r, q1_s, q1_r, q2_s, q2_r, z_s, z_r, near_sem, two_sem, four_sem,
):
    node, dp = lax.axis_index("node"), lax.axis_index("dp")
    x, yh, c = node // 4, (node // 2) % 2, node % 2
    z, yl = dp // 2, dp % 2
    y = yh * 2 + yl
    p = z % 2
    zs = (z + 17 - 2 * c) % NZ
    zup, zdn = (z + 1) % NZ, (z + 15) % NZ
    me = lambda **kw: device_at(kw.get("x", x), kw.get("y", y), kw.get("z", z), kw.get("c", c))

    def send(src, dst, ssem, rsem, to):
        return pltpu.make_async_remote_copy(
            src_ref=src, dst_ref=dst, send_sem=ssem, recv_sem=rsem, device_id=to, device_id_type=MESH
        )

    load_tok = pltpu.make_async_copy(tok_hbm, tok, load_sem.at[0])
    load_w = pltpu.make_async_copy(weight_hbm, shard, load_sem.at[1])
    load_vg = pltpu.make_async_copy(vg_hbm, vgall.at[pl.ds(0, T)], load_sem.at[2])
    load_gain = pltpu.make_async_copy(gain_hbm, gain_ref, load_sem.at[3])
    load_tok.start()
    load_w.start()
    load_vg.start()
    load_gain.start()

    barrier = pltpu.get_barrier_semaphore()
    partners = [me(x=(x + d) % NX) for d in (1, 2, 3)] + [me(y=(y + d) % NY) for d in (1, 2, 3)]
    partners += [me(c=1 - c), me(z=zup), me(z=zdn), me(z=zup, c=1 - c), me(z=zdn, c=1 - c)]
    for to in partners:
        pl.semaphore_signal(barrier, inc=1, device_id=to, device_id_type=MESH)

    def tell(sem, d):
        for to in (me(z=(z + d) % NZ), me(z=(z + NZ - d) % NZ)):
            pl.semaphore_signal(sem, inc=1, device_id=to, device_id_type=MESH)

    load_tok.wait()

    def squares(i, acc):
        t = tok[:, pl.ds(pl.multiple_of(i * K, K), K)].astype(F32)
        t = t * t
        return acc + ((t[:, 0:128] + t[:, 128:256]) + (t[:, 256:384] + t[:, 384:512]))

    acc = lax.fori_loop(0, D // K, squares, jnp.zeros((T, 128), F32))
    mean = jnp.sum(acc, axis=1, keepdims=True) * (1.0 / D)
    inv[...] = jnp.broadcast_to(lax.rsqrt(mean + EPS), (T, 128))

    def column(j, xt, ht):
        cc = c if j in (0, 2) else 1 - c
        pp = p if j < 2 else 1 - p
        return pl.multiple_of(xt * 2048 + ht * 1024 + cc * 512 + pp * 256, 256)

    def unit_tile(j, xt, ht):
        scale = inv[...]
        scale = jnp.concatenate([scale, scale], axis=1)
        return tok[:, pl.ds(column(j, xt, ht), F)].astype(F32) * scale

    load_w.wait()
    load_vg.wait()
    load_gain.wait()
    pl.semaphore_wait(barrier, len(partners))
    tell(near_sem, 1)

    slot = 3 - c
    helpers = [(me(c=1 - c), 1), (me(z=zs), slot), (me(z=zs, c=1 - c), slot)]

    def vg_copy(i, mine, to_slot, to):
        return send(
            vgall.at[pl.ds(mine * T, T)], vgall.at[pl.ds(to_slot * T, T)], vg_s.at[i], vg_r.at[to_slot - 1], to
        )

    vg_copies = [vg_copy(0, 0, 1, me(c=1 - c)), vg_copy(1, 0, slot, me(z=zs)), vg_copy(2, slot, slot, me(c=1 - c))]
    vg_copies[0].start()
    vg_copies[1].start()

    own_rows = pl.ds(pl.multiple_of(p * F, F), F)
    half = 1 - yl
    ax = [send(shard.at[own_rows], wall.at[x, yh], ax_s.at[d - 1], ax_r.at[d - 1], me(x=(x + d) % NX)) for d in (1, 2, 3)]
    out_half = pl.ds(pl.multiple_of(half * 128, 128), 128)
    in_half = pl.ds(pl.multiple_of(yl * 128, 128), 128)
    ay = [
        send(
            shard.at[pl.ds(pl.multiple_of(p * F + half * 128, 128), 128)] if d == 0 else wall.at[(x + d) % NX, yh, out_half],
            wall.at[(x + d) % NX, yh, out_half], ay_s.at[d], ay_r.at[d], me(y=3 - y),
        )
        for d in range(NX)
    ]
    ap = [
        send(
            wall.at[(x + d) % NX, 1 - yh, in_half], wall.at[(x + d) % NX, 1 - yh, in_half],
            ap_s.at[d], ap_r.at[d], me(y=yh * 2 + 1 - yl),
        )
        for d in range(NX)
    ]
    ay_in = [
        send(
            wall.at[(x + d) % NX, 1 - yh, in_half], wall.at[(x + d) % NX, 1 - yh, in_half],
            ay_s.at[d], ay_r.at[d], me(y=3 - y),
        )
        for d in range(NX)
    ]
    ay[0].start()
    ax[0].start()
    ax[2].start()
    ax[1].start()

    def token_copy(i, xt):
        to, sl = helpers[i]
        return send(
            nsend.at[i, xt], nall.at[xt, :, pl.ds(sl * T, T)], tok_s.at[i, xt], tok_r.at[sl - 1, xt], to
        )

    def normalize(m, carry):
        xt = (x + 2 + m) % NX
        for ht in range(2):
            for j in (2, 3, 1, 0):
                tile = unit_tile(j, xt, ht).astype(BF)
                if j == 0:
                    nall[xt, ht, 0:T] = tile
                else:
                    nsend[(0, 0, 1, 2)[j], xt, ht] = tile
        for i in (0, 1, 2):
            token_copy(i, xt).start()
        return carry

    lax.fori_loop(0, NX, normalize, 0)
    wall[x, yh] = shard[own_rows]

    vg_copy(1, 0, slot, me(z=zs)).wait_recv()
    vg_copies[2].start()
    pl.semaphore_wait(near_sem, 2)
    tell(two_sem, 2)
    for sl in (1, 2 + c):
        vg_copy(0, 0, sl, me(c=1 - c)).wait_recv()

    def p1_copy(d, ht):
        return send(
            s1.at[(x + d) % NX, pl.ds(ht * 2, 2)], r1.at[d - 1, pl.ds(ht * 2, 2)],
            p1_s.at[d - 1, ht], p1_r.at[d - 1, ht], me(x=(x + d) % NX),
        )

    def p2_copy(e, xt):
        return send(
            s2.at[(y + e) % NY, xt], r2.at[e - 1, xt], p2_s.at[e - 1, xt], p2_r.at[e - 1, xt], me(y=(y + e) % NY)
        )

    def weight_tile(xt, ht):
        total = lax.dot_general(nall[xt, ht], vgall[...], (((0,), (0,)), ((), ())), preferred_element_type=F32)
        total = total.astype(BF).reshape(8, 2, 16, K)
        for low in range(2):
            part = total[:, low].reshape(128, K)
            s1[xt, ht * 2 + low] = part[:, 0:256]
            s2[ht * 2 + low, xt] = part[:, 256:512]

    def weight_step(m):
        d = (2 + m) % NX
        xt = (x + d) % NX
        for sl in (1, 2, 3):
            send(nsend.at[0, xt], nall.at[xt, :, pl.ds(sl * T, T)], tok_s.at[0, xt], tok_r.at[sl - 1, xt], me(c=1 - c)).wait_recv()

        def tiles(h, carry):
            ht = (yh + 1 + h) % 2
            weight_tile(xt, ht)
            if d != 0:
                p1_copy(d, ht).start()
            for low in range(2):
                e = (ht * 2 + low - y + NY) % NY

                @pl.when(e != 0)
                def _():
                    p2_copy(e, xt).start()

            return carry

        lax.fori_loop(0, 2, tiles, 0)

    owners = [(me(c=1 - c), 1), (me(z=zup, c=1), 3 - c), (me(z=zdn, c=0), 2 + c)]

    def back_copy(i, xt, ht):
        to, j = owners[i]
        return send(
            ngs.at[xt, ht, pl.ds(i * T, T)], ngr.at[j, xt, ht], back_s.at[i, xt, ht], back_r.at[j - 1, xt, ht], to
        )

    def grad_tile(xt, ht):
        ng = lax.dot_general(
            vgall[...], wall[xt, ht], (((1,), (1,)), ((), ())), preferred_element_type=F32
        ).astype(BF)
        ngr[0, xt, ht] = ng[0:T]
        ngs[xt, ht] = ng[T:]
        for i in range(3):
            back_copy(i, xt, ht).start()

    weight_step(0)
    for i in (0, 2):
        ax[i].wait_recv()
    ay[3].start()
    ay[1].start()
    pl.semaphore_wait(two_sem, 2)
    tell(four_sem, 4)
    weight_step(1)
    ay_in[0].wait_recv()
    ap[0].start()
    ax[1].wait_recv()
    ay[2].start()
    weight_step(2)
    weight_step(3)
    for d in (1, 3):
        ay_in[d].wait_recv()
        ap[d].start()

    def near_tile(i, carry):
        grad_tile((x + i) % NX, yh)
        return carry

    lax.fori_loop(0, NX, near_tile, 0)
    ay_in[2].wait_recv()
    ap[2].start()

    def q1_copy(e):
        return send(t1.at[(y + e) % NY], u1.at[e - 1], q1_s.at[e - 1], q1_r.at[e - 1], me(y=(y + e) % NY))

    def q2_copy(d):
        return send(t2.at[(x + d) % NX], u2.at[d - 1], q2_s.at[d - 1], q2_r.at[d - 1], me(x=(x + d) % NX))

    for ht in range(2):
        for d in (1, 2, 3):
            p1_copy(d, ht).wait_recv()

    def add1(e, carry):
        yt = (y + e) % NY
        total = s1[x, yt].astype(F32) + r1[0, yt].astype(F32) + r1[1, yt].astype(F32) + r1[2, yt].astype(F32)
        t1[yt] = total.astype(BF)

        @pl.when(e != NY)
        def _():
            q1_copy(e).start()

        return carry

    lax.fori_loop(1, NY + 1, add1, 0)
    for xt in range(NX):
        for e in (1, 2, 3):
            p2_copy(e, xt).wait_recv()

    def add2(d, carry):
        xt = (x + d) % NX
        total = s2[y, xt].astype(F32) + r2[0, xt].astype(F32) + r2[1, xt].astype(F32) + r2[2, xt].astype(F32)
        t2[xt] = total.astype(BF)

        @pl.when(d != NX)
        def _():
            q2_copy(d).start()

        return carry

    lax.fori_loop(1, NX + 1, add2, 0)

    for d in (0, 1, 3, 2):
        send(
            wall.at[(x + d) % NX, 1 - yh, out_half], wall.at[(x + d) % NX, 1 - yh, out_half],
            ap_s.at[d], ap_r.at[d], me(y=yh * 2 + 1 - yl),
        ).wait_recv()

    def far_tile(i, carry):
        grad_tile((x + i) % NX, 1 - yh)
        return carry

    lax.fori_loop(0, NX, far_tile, 0)

    for e in (1, 2, 3):
        q1_copy(e).wait_recv()
    total = t1[y].astype(F32) + u1[0].astype(F32) + u1[1].astype(F32) + u1[2].astype(F32)
    vb[:, :, 0:256] = total.astype(BF).reshape(8, 16, 256)
    for d in (1, 2, 3):
        q2_copy(d).wait_recv()
    total = t2[x].astype(F32) + u2[0].astype(F32) + u2[1].astype(F32) + u2[2].astype(F32)
    vb[:, :, 256:512] = total.astype(BF).reshape(8, 16, 256)

    pl.semaphore_wait(four_sem, 2)

    def z_copy(k):
        return send(vb.at[k], zr.at[z // 2], z_s.at[k], z_r.at[z // 2], me(z=p * 8 + k))

    def z_start(i, carry):
        k = (z + i) % 8

        @pl.when(p * 8 + k != z)
        def _():
            z_copy(k).start()

        @pl.when(p * 8 + k == z)
        def _():
            zr[z // 2] = vb[k]

        return carry

    lax.fori_loop(0, 8, z_start, 0)

    for j in (1, 2, 3):
        for xt in range(NX):
            for ht in range(2):
                send(
                    ngs.at[xt, ht, pl.ds(0, T)], ngr.at[j, xt, ht],
                    back_s.at[0, xt, ht], back_r.at[j - 1, xt, ht], me(c=1 - c),
                ).wait_recv()

    def feature_tile(j, xt, ht):
        return ngr[j, xt, ht].astype(F32) * gain_ref[:, pl.ds(column(j, xt, ht), F)]

    def spread_tile(i, acc):
        xt, ht = i // 2, i % 2
        for j in range(4):
            prod = feature_tile(j, xt, ht) * unit_tile(j, xt, ht)
            acc = acc + (prod[:, 0:128] + prod[:, 128:256])
        return acc

    acc = lax.fori_loop(0, 8, spread_tile, jnp.zeros((T, 128), F32))
    spread = jnp.sum(acc, axis=1, keepdims=True) * (1.0 / D)

    def input_tile(i, carry):
        xt, ht = i // 2, i % 2
        scale = inv[...]
        scale = jnp.concatenate([scale, scale], axis=1)
        for j in range(4):
            grad = scale * (feature_tile(j, xt, ht) - unit_tile(j, xt, ht) * spread)
            ig_ref[:, pl.ds(column(j, xt, ht), F)] = grad.astype(BF)
        return carry

    lax.fori_loop(0, 8, input_tile, 0)

    def z_wait(k, carry):
        @pl.when(2 * k + z // 8 != z)
        def _():
            send(vb.at[k], zr.at[k], z_s.at[k], z_r.at[k], me(z=(z + 1) % NZ)).wait_recv()

        return carry

    lax.fori_loop(0, 8, z_wait, 0)
    total = zr[0].astype(F32)
    for k in range(1, 8):
        total = total + zr[k].astype(F32)

    lanes = lax.broadcasted_iota(jnp.int32, (16, 128), 1)
    rows = lax.broadcasted_iota(jnp.int32, (16, 128), 0)
    block = gain_ref[:, pl.ds(pl.multiple_of(node * 512 + (dp // 8) * 128, 128), 128)]
    picked = jnp.where(lanes == rows + (dp % 8) * 16, jnp.broadcast_to(block, (16, 128)), 0.0)
    wg_ref[...] = total * jnp.sum(picked, axis=1, keepdims=True)
    own = shard[pl.ds(pl.multiple_of(dp * 16, 16), 16)].astype(F32)
    gain_sum = jnp.sum(own * total, axis=1, keepdims=True)
    spread_out = jnp.where(lanes == rows, jnp.broadcast_to(gain_sum, (16, 128)), 0.0)
    gg_ref[...] = jnp.sum(spread_out, axis=0, keepdims=True)

    for copy in vg_copies + ax + ay + ap:
        copy.wait_send()
    for i in range(3):
        for xt in range(NX):
            token_copy(i, xt).wait_send()
            for ht in range(2):
                back_copy(i, xt, ht).wait_send()
            p2_copy(i + 1, xt).wait_send()
        for ht in range(2):
            p1_copy(i + 1, ht).wait_send()
        q1_copy(i + 1).wait_send()
        q2_copy(i + 1).wait_send()

    def z_sent(k, carry):
        @pl.when(p * 8 + k != z)
        def _():
            z_copy(k).wait_send()

        return carry

    lax.fori_loop(0, 8, z_sent, 0)


def on_device(tokens_in, gain, value_weight, value_grad):
    vmem, dma = pltpu.VMEM, pltpu.SemaphoreType.DMA
    scratch = [
        vmem((T, D), BF), vmem((1, D), F32), vmem((K, K), BF), vmem((4 * T, K), BF), vmem((T, 128), F32),
        vmem((3, NX, 2, T, F), BF), vmem((NX, 2, 4 * T, F), BF), vmem((NX, 2, F, K), BF),
        vmem((NX, 2, 3 * T, F), BF), vmem((4, NX, 2, T, F), BF),
        vmem((NX, NY, 128, 256), BF), vmem((NY, NX, 128, 256), BF),
        vmem((3, NY, 128, 256), BF), vmem((3, NX, 128, 256), BF),
        vmem((NY, 128, 256), BF), vmem((NX, 128, 256), BF),
        vmem((3, 128, 256), BF), vmem((3, 128, 256), BF),
        vmem((8, 16, K), BF), vmem((8, 16, K), BF),
    ]
    sems = [(4,)] + [(3,)] * 2 + [(3, NX)] * 2 + [(3,)] * 2 + [(4,)] * 4 + [(3, NX, 2)] * 2
    sems += [(3, 2)] * 2 + [(3, NX)] * 2 + [(3,)] * 4 + [(8,)] * 2
    in_hbm = pl.BlockSpec(memory_space=pltpu.HBM)
    in_vmem = pl.BlockSpec(memory_space=pltpu.VMEM)
    weight_grad, gain_grad, input_grad = pl.pallas_call(
        kernel,
        out_shape=(
            jax.ShapeDtypeStruct((16, K), F32),
            jax.ShapeDtypeStruct((1, 128), F32),
            jax.ShapeDtypeStruct((T, D), BF),
        ),
        in_specs=[in_hbm] * 4,
        out_specs=(in_vmem, in_vmem, in_vmem),
        scratch_shapes=scratch + [dma(s) for s in sems] + [pltpu.SemaphoreType.REGULAR] * 3,
        compiler_params=pltpu.CompilerParams(
            collective_id=0, has_side_effects=True, vmem_limit_bytes=40 * 1024 * 1024
        ),
    )(*(pltpu.with_memory_space_constraint(a, pltpu.HBM) for a in (tokens_in, gain.reshape(1, D), value_weight, value_grad)))
    return weight_grad, gain_grad[0, :16], input_grad


def solution(mesh):
    placed = (P(("node", "dp"), None), P(), P("node", None), P(("node", "dp"), None))
    return jax.shard_map(
        on_device,
        mesh=mesh,
        in_specs=placed,
        out_specs=(P(("node", "dp"), None), P(("node", "dp")), P(("node", "dp"), None)),
        check_vma=False,
    )
```

```python
import jax
import jax.numpy as jnp
from jax import lax
from jax.experimental import pallas as pl
from jax.experimental.pallas import tpu as pltpu
from jax.sharding import PartitionSpec as P

D = 8192
EPS = 1e-05
NX, NY, NZ = 4, 4, 16
T = 128
K = 512
F = 256
BF, F32 = jnp.bfloat16, jnp.float32
MESH = pl.DeviceIdType.MESH
STEPS = (2, 0, 3, 1)


def device_at(x, y, z, core):
    return (x * 4 + (y // 2) * 2 + core, z * 2 + y % 2)


def kernel(
    tok_hbm, gain_hbm, weight_hbm, vg_hbm,
    wg_ref, gg_ref, ig_ref,
    tok, gain_ref, shard, vgraw, vgall, nall, wall, ngs, ngr,
    s1, s2, a1, a2, r1, r2, t1, t2, u1, u2, vb, zr,
    load_sem, vg_s, vg_r, tok_s, tok_r, ax_s, ax_r, ay_s, ay_r, ap_s, ap_r,
    back_s, back_r, a1_s, a1_r, a2_s, a2_r, p1_s, p1_r, p2_s, p2_r, q1_s, q1_r, q2_s, q2_r, z_s, z_r, near_sem, two_sem, four_sem,
):
    node, dp = lax.axis_index("node"), lax.axis_index("dp")
    x, yh, c = node // 4, (node // 2) % 2, node % 2
    z, yl = dp // 2, dp % 2
    y = yh * 2 + yl
    p = z % 2
    zs = (z + 17 - 2 * c) % NZ
    zup, zdn = (z + 1) % NZ, (z + 15) % NZ
    me = lambda **kw: device_at(kw.get("x", x), kw.get("y", y), kw.get("z", z), kw.get("c", c))

    def send(src, dst, ssem, rsem, to):
        return pltpu.make_async_remote_copy(
            src_ref=src, dst_ref=dst, send_sem=ssem, recv_sem=rsem, device_id=to, device_id_type=MESH
        )

    load_tok = pltpu.make_async_copy(tok_hbm, tok, load_sem.at[0])
    load_w = pltpu.make_async_copy(weight_hbm, shard, load_sem.at[1])
    load_vg = pltpu.make_async_copy(vg_hbm, vgraw, load_sem.at[2])
    load_gain = pltpu.make_async_copy(gain_hbm, gain_ref, load_sem.at[3])
    load_w.start()
    load_tok.start()
    load_vg.start()
    load_gain.start()

    barrier = pltpu.get_barrier_semaphore()
    partners = [me(x=(x + d) % NX) for d in (1, 2, 3)] + [me(y=(y + d) % NY) for d in (1, 2, 3)]
    partners += [me(c=1 - c), me(z=zup), me(z=zdn), me(z=zup, c=1 - c), me(z=zdn, c=1 - c)]
    for to in partners:
        pl.semaphore_signal(barrier, inc=1, device_id=to, device_id_type=MESH)

    def tell(sem, d):
        for to in (me(z=(z + d) % NZ), me(z=(z + NZ - d) % NZ)):
            pl.semaphore_signal(sem, inc=1, device_id=to, device_id_type=MESH)

    def column(j, xt, ht):
        cc = c if j in (0, 2) else 1 - c
        pp = p if j < 2 else 1 - p
        return pl.multiple_of(xt * 2048 + ht * 1024 + cc * 512 + pp * 256, 256)

    load_w.wait()
    pl.semaphore_wait(barrier, len(partners))
    tell(near_sem, 1)

    own_rows = pl.ds(pl.multiple_of(p * F, F), F)
    half = 1 - yl
    out_half = pl.ds(pl.multiple_of(half * 128, 128), 128)
    in_half = pl.ds(pl.multiple_of(yl * 128, 128), 128)
    def shard_half(h):
        return shard.at[pl.ds(pl.multiple_of(p * F + h * 128, 128), 128)]

    axo, axi = [
        [
            send(shard_half(h), wall.at[x, yh, rows], ax_s.at[k, d - 1], ax_r.at[k, d - 1], me(x=(x + d) % NX))
            for d in (1, 2, 3)
        ]
        for k, (h, rows) in enumerate(((half, out_half), (yl, in_half)))
    ]
    ay = [
        send(
            shard.at[own_rows] if d == 0 else wall.at[(x + d) % NX, yh, out_half],
            wall.at[x, yh] if d == 0 else wall.at[(x + d) % NX, yh, out_half], ay_s.at[d], ay_r.at[d], me(y=3 - y),
        )
        for d in range(NX)
    ]
    ap = {
        d: send(
            wall.at[(x + d) % NX, 1 - yh, in_half], wall.at[(x + d) % NX, 1 - yh, in_half],
            ap_s.at[d], ap_r.at[d], me(y=yh * 2 + 1 - yl),
        )
        for d in (1, 2, 3)
    }
    ay_in = [
        send(
            wall.at[x, 1 - yh] if d == 0 else wall.at[(x + d) % NX, 1 - yh, in_half],
            wall.at[x, 1 - yh] if d == 0 else wall.at[(x + d) % NX, 1 - yh, in_half],
            ay_s.at[d], ay_r.at[d], me(y=3 - y),
        )
        for d in range(NX)
    ]

    slot = 3 - c
    helpers = [(me(c=1 - c), 1), (me(z=zs), slot), (me(z=zs, c=1 - c), slot)]

    def token_copy(i, xt, ht):
        to, sl = helpers[i]
        return send(
            tok_hbm.at[:, pl.ds(column(i + 1, xt, ht), F)], nall.at[xt, ht, pl.ds(sl * T, T)],
            tok_s.at[i, xt, ht], tok_r.at[sl - 1, xt, ht], to,
        )

    def token_sends(m, carry):
        xt = (x + STEPS[m]) % NX
        for ht in range(2):
            for i in range(3):
                token_copy(i, xt, ht).start()
        return carry

    token_sends(0, 0)
    ay[0].start()
    for i in (0, 2, 1):
        axo[i].start()
    load_tok.wait()

    def squares(i, acc):
        t = tok[:, pl.ds(pl.multiple_of(i * K, K), K)].astype(F32)
        t = t * t
        return acc + ((t[:, 0:128] + t[:, 128:256]) + (t[:, 256:384] + t[:, 384:512]))

    acc = lax.fori_loop(0, D // K, squares, jnp.zeros((T, 128), F32))
    mean_square = jnp.sum(acc, axis=1, keepdims=True) * (1.0 / D)
    inv_rms = lax.rsqrt(mean_square + EPS)
    load_vg.wait()
    vgall[0:T] = (vgraw[...].astype(F32) * inv_rms).astype(BF)

    def vg_copy(i, mine, to_slot, to):
        return send(
            vgall.at[pl.ds(mine * T, T)], vgall.at[pl.ds(to_slot * T, T)], vg_s.at[i], vg_r.at[to_slot - 1], to
        )

    vg_copies = [vg_copy(0, 0, 1, me(c=1 - c)), vg_copy(1, 0, slot, me(z=zs)), vg_copy(2, slot, slot, me(c=1 - c))]
    vg_copies[0].start()
    vg_copies[1].start()
    token_sends(1, 0)
    wall[x, yh] = shard[own_rows]

    def own_tokens(i, carry):
        nall[i // 2, i % 2, 0:T] = tok[:, pl.ds(column(0, i // 2, i % 2), F)]
        return carry

    lax.fori_loop(0, 8, own_tokens, 0)
    load_gain.wait()

    axo[0].wait_recv()
    ay[3].start()
    axo[2].wait_recv()
    ay[1].start()
    token_sends(2, 0)
    axi[0].start()
    axi[2].start()

    vg_copy(1, 0, slot, me(z=zs)).wait_recv()
    vg_copies[2].start()
    pl.semaphore_wait(near_sem, 2)
    tell(two_sem, 2)
    for sl in (1, 2 + c):
        vg_copy(0, 0, sl, me(c=1 - c)).wait_recv()

    def a1_copy(ht):
        return send(
            s1.at[(x + 2) % NX, pl.ds(ht * 2, 2)], a1.at[ht], a1_s.at[ht], a1_r.at[ht], me(x=(x + (1, 3)[ht]) % NX)
        )

    def a2_copy(m):
        xt = (x + STEPS[m]) % NX
        return send(s2.at[(y + 2) % NY, xt], a2.at[m], a2_s.at[m], a2_r.at[m], me(y=(y + (1, 3)[m % 2]) % NY))

    def p1_copy(d, ht):
        return send(
            s1.at[(x + d) % NX, pl.ds(ht * 2, 2)], r1.at[d // 2, pl.ds(ht * 2, 2)],
            p1_s.at[d // 2, ht], p1_r.at[d // 2, ht], me(x=(x + d) % NX),
        )

    def p2_copy(e, m):
        xt = (x + STEPS[m]) % NX
        return send(
            s2.at[(y + e) % NY, xt], r2.at[e // 2, xt], p2_s.at[e // 2, m], p2_r.at[e // 2, m], me(y=(y + e) % NY)
        )

    def weight_tile(xt, ht):
        total = lax.dot_general(nall[xt, ht], vgall[...], (((0,), (0,)), ((), ())), preferred_element_type=F32)
        total = total.astype(BF).reshape(8, 2, 16, K)
        for low in range(2):
            part = total[:, low].reshape(128, K)
            s1[xt, ht * 2 + low] = part[:, 0:256]
            s2[ht * 2 + low, xt] = part[:, 256:512]

    def weight_step(m):
        d = STEPS[m]
        xt = (x + d) % NX
        for ht in range(2):
            for sl in (1, 2, 3):
                send(
                    nall.at[xt, ht, pl.ds(0, T)], nall.at[xt, ht, pl.ds(sl * T, T)],
                    tok_s.at[0, xt, ht], tok_r.at[sl - 1, xt, ht], me(c=1 - c),
                ).wait_recv()
            weight_tile(xt, ht)
            if d == 2:
                a1_copy(ht).start()
            elif d != 0:
                if (d, ht) in ((1, 0), (3, 1)):
                    a1_copy(ht).wait_recv()
                    rows = pl.ds(ht * 2, 2)
                    s1[xt, rows] = (s1[xt, rows].astype(F32) + a1[ht].astype(F32)).astype(BF)
                p1_copy(d, ht).start()
        a2_copy(m).start()
        p2_copy((3, 1)[m % 2], m).start()

    def relay(m):
        e, xt = (1, 3)[m % 2], (x + STEPS[m]) % NX
        yt = (y + e) % NY
        a2_copy(m).wait_recv()
        s2[yt, xt] = (s2[yt, xt].astype(F32) + a2[m].astype(F32)).astype(BF)
        p2_copy(e, m).start()

    owners = [(me(c=1 - c), 1), (me(z=zup, c=1), 3 - c), (me(z=zdn, c=0), 2 + c)]

    def back_copy(i, xt, ht):
        to, j = owners[i]
        return send(
            ngs.at[xt, ht, pl.ds(i * T, T)], ngr.at[j, xt, ht], back_s.at[i, xt, ht], back_r.at[j - 1, xt, ht], to
        )

    def grad_tile(xt, ht):
        ng = lax.dot_general(
            vgall[...], wall[xt, ht], (((1,), (1,)), ((), ())), preferred_element_type=F32
        ).astype(BF)
        ngr[0, xt, ht] = ng[0:T]
        ngs[xt, ht] = ng[T:]
        for i in range(3):
            back_copy(i, xt, ht).start()

    weight_step(0)
    token_sends(3, 0)
    pl.semaphore_wait(two_sem, 2)
    tell(four_sem, 4)
    axo[1].wait_recv()
    ay[2].start()
    axi[1].start()
    weight_step(1)
    ay_in[3].wait_recv()
    ap[3].start()
    weight_step(2)
    relay(0)
    ay_in[1].wait_recv()
    ap[1].start()
    weight_step(3)
    relay(1)
    ay_in[2].wait_recv()
    ap[2].start()
    for copy in axi:
        copy.wait_recv()

    def near_tile(i, carry):
        grad_tile((x + i) % NX, yh)
        return carry

    lax.fori_loop(0, NX, near_tile, 0)
    ay_in[0].wait_recv()
    grad_tile(x, 1 - yh)

    def q1_copy(e):
        return send(t1.at[(y + e) % NY], u1.at[e - 1], q1_s.at[e - 1], q1_r.at[e - 1], me(y=(y + e) % NY))

    def q2_copy(d):
        return send(t2.at[(x + d) % NX], u2.at[d - 1], q2_s.at[d - 1], q2_r.at[d - 1], me(x=(x + d) % NX))

    for m in (2, 3):
        relay(m)
    for ht in range(2):
        for d in (1, 3):
            p1_copy(d, ht).wait_recv()

    def add1(e, carry):
        yt = (y + e) % NY
        total = s1[x, yt].astype(F32) + r1[0, yt].astype(F32) + r1[1, yt].astype(F32)
        t1[yt] = total.astype(BF)

        @pl.when(e != NY)
        def _():
            q1_copy(e).start()

        return carry

    lax.fori_loop(1, NY + 1, add1, 0)
    for m in range(NX):
        for e in (1, 3):
            p2_copy(e, m).wait_recv()

    def add2(d, carry):
        xt = (x + d) % NX
        total = s2[y, xt].astype(F32) + r2[0, xt].astype(F32) + r2[1, xt].astype(F32)
        t2[xt] = total.astype(BF)

        @pl.when(d != NX)
        def _():
            q2_copy(d).start()

        return carry

    lax.fori_loop(1, NX + 1, add2, 0)

    for d in (3, 1, 2):
        send(
            wall.at[(x + d) % NX, 1 - yh, out_half], wall.at[(x + d) % NX, 1 - yh, out_half],
            ap_s.at[d], ap_r.at[d], me(y=yh * 2 + 1 - yl),
        ).wait_recv()
        grad_tile((x + d) % NX, 1 - yh)

    for e in (1, 2, 3):
        q1_copy(e).wait_recv()
    total = t1[y].astype(F32) + u1[0].astype(F32) + u1[1].astype(F32) + u1[2].astype(F32)
    vb[:, :, 0:256] = total.astype(BF).reshape(8, 16, 256)
    for d in (1, 2, 3):
        q2_copy(d).wait_recv()
    total = t2[x].astype(F32) + u2[0].astype(F32) + u2[1].astype(F32) + u2[2].astype(F32)
    vb[:, :, 256:512] = total.astype(BF).reshape(8, 16, 256)

    pl.semaphore_wait(four_sem, 2)

    def z_copy(k):
        return send(vb.at[k], zr.at[z // 2], z_s.at[k], z_r.at[z // 2], me(z=p * 8 + k))

    def z_start(i, carry):
        k = (z + i) % 8

        @pl.when(p * 8 + k != z)
        def _():
            z_copy(k).start()

        @pl.when(p * 8 + k == z)
        def _():
            zr[z // 2] = vb[k]

        return carry

    lax.fori_loop(0, 8, z_start, 0)

    for j in (1, 2, 3):
        for xt in range(NX):
            for ht in range(2):
                send(
                    ngs.at[xt, ht, pl.ds(0, T)], ngr.at[j, xt, ht],
                    back_s.at[0, xt, ht], back_r.at[j - 1, xt, ht], me(c=1 - c),
                ).wait_recv()

    def feature_tile(j, xt, ht):
        return ngr[j, xt, ht].astype(F32) * gain_ref[:, pl.ds(column(j, xt, ht), F)]

    def token_tile(j, xt, ht):
        return tok[:, pl.ds(column(j, xt, ht), F)].astype(F32)

    def spread_tile(i, acc):
        xt, ht = i // 2, i % 2
        for j in range(4):
            prod = feature_tile(j, xt, ht) * token_tile(j, xt, ht)
            acc = acc + (prod[:, 0:128] + prod[:, 128:256])
        return acc

    acc = lax.fori_loop(0, 8, spread_tile, jnp.zeros((T, 128), F32))
    spread = jnp.sum(acc, axis=1, keepdims=True) * (1.0 / D) * (inv_rms * inv_rms)

    def input_tile(i, carry):
        xt, ht = i // 2, i % 2
        for j in range(4):
            grad = feature_tile(j, xt, ht) - token_tile(j, xt, ht) * spread
            ig_ref[:, pl.ds(column(j, xt, ht), F)] = grad.astype(BF)
        return carry

    lax.fori_loop(0, 8, input_tile, 0)

    def z_wait(k, carry):
        @pl.when(2 * k + z // 8 != z)
        def _():
            send(vb.at[k], zr.at[k], z_s.at[k], z_r.at[k], me(z=(z + 1) % NZ)).wait_recv()

        return carry

    lax.fori_loop(0, 8, z_wait, 0)
    total = zr[0].astype(F32)
    for k in range(1, 8):
        total = total + zr[k].astype(F32)

    lanes = lax.broadcasted_iota(jnp.int32, (16, 128), 1)
    rows = lax.broadcasted_iota(jnp.int32, (16, 128), 0)
    block = gain_ref[:, pl.ds(pl.multiple_of(node * 512 + (dp // 8) * 128, 128), 128)]
    picked = jnp.where(lanes == rows + (dp % 8) * 16, jnp.broadcast_to(block, (16, 128)), 0.0)
    wg_ref[...] = total * jnp.sum(picked, axis=1, keepdims=True)
    own = shard[pl.ds(pl.multiple_of(dp * 16, 16), 16)].astype(F32)
    gain_sum = jnp.sum(own * total, axis=1, keepdims=True)
    spread_out = jnp.where(lanes == rows, jnp.broadcast_to(gain_sum, (16, 128)), 0.0)
    gg_ref[...] = jnp.sum(spread_out, axis=0, keepdims=True)

    for copy in vg_copies + axo + axi + ay + [ap[1], ap[2], ap[3]]:
        copy.wait_send()
    for i in range(3):
        for xt in range(NX):
            for ht in range(2):
                token_copy(i, xt, ht).wait_send()
                back_copy(i, xt, ht).wait_send()
        q1_copy(i + 1).wait_send()
        q2_copy(i + 1).wait_send()

    for ht in range(2):
        a1_copy(ht).wait_send()
        for d in (1, 3):
            p1_copy(d, ht).wait_send()
    for m in range(NX):
        a2_copy(m).wait_send()
        for e in (1, 3):
            p2_copy(e, m).wait_send()

    def z_sent(k, carry):
        @pl.when(p * 8 + k != z)
        def _():
            z_copy(k).wait_send()

        return carry

    lax.fori_loop(0, 8, z_sent, 0)


def on_device(tokens_in, gain, value_weight, value_grad):
    vmem, dma = pltpu.VMEM, pltpu.SemaphoreType.DMA
    scratch = [
        vmem((T, D), BF), vmem((1, D), F32), vmem((K, K), BF), vmem((T, K), BF), vmem((4 * T, K), BF),
        vmem((NX, 2, 4 * T, F), BF), vmem((NX, 2, F, K), BF),
        vmem((NX, 2, 3 * T, F), BF), vmem((4, NX, 2, T, F), BF),
        vmem((NX, NY, 128, 256), BF), vmem((NY, NX, 128, 256), BF),
        vmem((2, 2, 128, 256), BF), vmem((NX, 128, 256), BF),
        vmem((2, NY, 128, 256), BF), vmem((2, NX, 128, 256), BF),
        vmem((NY, 128, 256), BF), vmem((NX, 128, 256), BF),
        vmem((3, 128, 256), BF), vmem((3, 128, 256), BF),
        vmem((8, 16, K), BF), vmem((8, 16, K), BF),
    ]
    sems = [(4,)] + [(3,)] * 2 + [(3, NX, 2)] * 2 + [(2, 3)] * 2 + [(4,)] * 4 + [(3, NX, 2)] * 2
    sems += [(2,)] * 2 + [(NX,)] * 2 + [(2, 2)] * 2 + [(2, NX)] * 2 + [(3,)] * 4 + [(8,)] * 2
    operands = (tokens_in, gain.reshape(1, D), value_weight, value_grad)
    operands = [pltpu.with_memory_space_constraint(a, pltpu.HBM) for a in operands]
    in_hbm = pl.BlockSpec(memory_space=pltpu.HBM)
    in_vmem = pl.BlockSpec(memory_space=pltpu.VMEM)
    weight_grad, gain_grad, input_grad = pl.pallas_call(
        kernel,
        out_shape=(
            jax.ShapeDtypeStruct((16, K), F32),
            jax.ShapeDtypeStruct((1, 128), F32),
            jax.ShapeDtypeStruct((T, D), BF),
        ),
        in_specs=[in_hbm] * 4,
        out_specs=(in_vmem, in_vmem, in_vmem),
        scratch_shapes=scratch + [dma(s) for s in sems] + [pltpu.SemaphoreType.REGULAR] * 3,
        compiler_params=pltpu.CompilerParams(
            collective_id=0, has_side_effects=True, vmem_limit_bytes=40 * 1024 * 1024
        ),
    )(*operands)
    return weight_grad, gain_grad[0, :16], input_grad


def solution(mesh):
    placed = (P(("node", "dp"), None), P(), P("node", None), P(("node", "dp"), None))
    return jax.shard_map(
        on_device,
        mesh=mesh,
        in_specs=placed,
        out_specs=(P(("node", "dp"), None), P(("node", "dp")), P(("node", "dp"), None)),
        check_vma=False,
    )
```

```python
import jax
import jax.numpy as jnp
from jax import lax
from jax.experimental import pallas as pl
from jax.experimental.pallas import tpu as pltpu
from jax.sharding import PartitionSpec as P

D = 8192
EPS = 1e-05
NX, NY, NZ = 4, 4, 16
T = 128
K = 512
F = 256
BF, F32 = jnp.bfloat16, jnp.float32
MESH = pl.DeviceIdType.MESH
STEPS = (2, 0, 3, 1)


def device_at(x, y, z, core):
    return (x * 4 + (y // 2) * 2 + core, z * 2 + y % 2)


def kernel(
    tok_hbm, gain_hbm, weight_hbm, vg_hbm,
    wg_ref, gg_ref, ig_ref,
    tok, gain_ref, shard, vgraw, vgall, invs, nall, wall, ngs, ngr,
    s1, s2, a1, a2, r1, r2, t1, t2, u1, u2, vb, zr,
    load_sem, vg_s, vg_r, inv_s, inv_r, tok_s, tok_r, ax_s, ax_r, ay_s, ay_r, ap_s, ap_r,
    back_s, back_r, a1_s, a1_r, a2_s, a2_r, p1_s, p1_r, p2_s, p2_r, q1_s, q1_r, q2_s, q2_r, z_s, z_r, near_sem, two_sem, four_sem,
):
    node, dp = lax.axis_index("node"), lax.axis_index("dp")
    x, yh, c = node // 4, (node // 2) % 2, node % 2
    z, yl = dp // 2, dp % 2
    y = yh * 2 + yl
    p = z % 2
    zs = (z + 17 - 2 * c) % NZ
    zup, zdn = (z + 1) % NZ, (z + 15) % NZ
    me = lambda **kw: device_at(kw.get("x", x), kw.get("y", y), kw.get("z", z), kw.get("c", c))

    def send(src, dst, ssem, rsem, to):
        return pltpu.make_async_remote_copy(
            src_ref=src, dst_ref=dst, send_sem=ssem, recv_sem=rsem, device_id=to, device_id_type=MESH
        )

    load_tok = pltpu.make_async_copy(tok_hbm, tok, load_sem.at[0])
    load_w = pltpu.make_async_copy(weight_hbm, shard, load_sem.at[1])
    load_vg = pltpu.make_async_copy(vg_hbm, vgraw.at[pl.ds(0, T)], load_sem.at[2])
    load_gain = pltpu.make_async_copy(gain_hbm, gain_ref, load_sem.at[3])
    load_vg.start()
    load_w.start()
    load_tok.start()
    load_gain.start()

    barrier = pltpu.get_barrier_semaphore()
    partners = [me(x=(x + d) % NX) for d in (1, 2, 3)] + [me(y=(y + d) % NY) for d in (1, 2, 3)]
    partners += [me(c=1 - c), me(z=zup), me(z=zdn), me(z=zup, c=1 - c), me(z=zdn, c=1 - c)]
    for to in partners:
        pl.semaphore_signal(barrier, inc=1, device_id=to, device_id_type=MESH)

    def tell(sem, d):
        for to in (me(z=(z + d) % NZ), me(z=(z + NZ - d) % NZ)):
            pl.semaphore_signal(sem, inc=1, device_id=to, device_id_type=MESH)

    def column(j, xt, ht):
        cc = c if j in (0, 2) else 1 - c
        pp = p if j < 2 else 1 - p
        return pl.multiple_of(xt * 2048 + ht * 1024 + cc * 512 + pp * 256, 256)

    load_w.wait()
    pl.semaphore_wait(barrier, len(partners))
    tell(near_sem, 1)

    own_rows = pl.ds(pl.multiple_of(p * F, F), F)
    half = 1 - yl
    out_half = pl.ds(pl.multiple_of(half * 128, 128), 128)
    in_half = pl.ds(pl.multiple_of(yl * 128, 128), 128)
    def shard_half(h):
        return shard.at[pl.ds(pl.multiple_of(p * F + h * 128, 128), 128)]

    axo, axi = [
        [
            send(shard_half(h), wall.at[x, yh, rows], ax_s.at[k, d - 1], ax_r.at[k, d - 1], me(x=(x + d) % NX))
            for d in (1, 2, 3)
        ]
        for k, (h, rows) in enumerate(((half, out_half), (yl, in_half)))
    ]
    ay = [
        send(
            shard.at[own_rows] if d == 0 else wall.at[(x + d) % NX, yh, out_half],
            wall.at[x, yh] if d == 0 else wall.at[(x + d) % NX, yh, out_half], ay_s.at[d], ay_r.at[d], me(y=3 - y),
        )
        for d in range(NX)
    ]
    ap = {
        d: send(
            wall.at[(x + d) % NX, 1 - yh, in_half], wall.at[(x + d) % NX, 1 - yh, in_half],
            ap_s.at[d], ap_r.at[d], me(y=yh * 2 + 1 - yl),
        )
        for d in (1, 2, 3)
    }
    ay_in = [
        send(
            wall.at[x, 1 - yh] if d == 0 else wall.at[(x + d) % NX, 1 - yh, in_half],
            wall.at[x, 1 - yh] if d == 0 else wall.at[(x + d) % NX, 1 - yh, in_half],
            ay_s.at[d], ay_r.at[d], me(y=3 - y),
        )
        for d in range(NX)
    ]

    slot = 3 - c
    helpers = [(me(c=1 - c), 1), (me(z=zs), slot), (me(z=zs, c=1 - c), slot)]

    def token_copy(i, xt, ht):
        to, sl = helpers[i]
        return send(
            tok_hbm.at[:, pl.ds(column(i + 1, xt, ht), F)], nall.at[xt, ht, pl.ds(sl * T, T)],
            tok_s.at[i, xt, ht], tok_r.at[sl - 1, xt, ht], to,
        )

    def token_sends(m, tiles=(0, 1)):
        xt = (x + STEPS[m]) % NX
        for ht in tiles:
            for i in range(3):
                token_copy(i, xt, ht).start()

    def vg_copy(i, mine, to_slot, to):
        return send(
            vgraw.at[pl.ds(mine * T, T)], vgraw.at[pl.ds(to_slot * T, T)], vg_s.at[i], vg_r.at[to_slot - 1], to
        )

    def inv_copy(i):
        to, sl = helpers[i]
        return send(invs.at[0], invs.at[sl], inv_s.at[i], inv_r.at[sl - 1], to)

    vg_copies = [vg_copy(0, 0, 1, me(c=1 - c)), vg_copy(1, 0, slot, me(z=zs)), vg_copy(2, slot, slot, me(c=1 - c))]
    load_vg.wait()
    vg_copies[0].start()
    vg_copies[1].start()
    token_sends(0, (0,))
    ay[0].start()
    for i in (0, 2, 1):
        axo[i].start()
    load_tok.wait()

    def squares(i, acc):
        t = tok[:, pl.ds(pl.multiple_of(i * K, K), K)].astype(F32)
        t = t * t
        return acc + ((t[:, 0:128] + t[:, 128:256]) + (t[:, 256:384] + t[:, 384:512]))

    acc = lax.fori_loop(0, D // K, squares, jnp.zeros((T, 128), F32))
    mean_square = jnp.sum(acc, axis=1, keepdims=True) * (1.0 / D)
    inv_rms = lax.rsqrt(mean_square + EPS)
    invs[0] = jnp.broadcast_to(inv_rms, (T, 128)).T[0:8]
    for i in range(3):
        inv_copy(i).start()
    token_sends(0, (1,))
    token_sends(1)
    wall[x, yh] = shard[own_rows]

    def own_tokens(i, carry):
        nall[i // 2, i % 2, 0:T] = tok[:, pl.ds(column(0, i // 2, i % 2), F)]
        return carry

    lax.fori_loop(0, 8, own_tokens, 0)
    load_gain.wait()

    vg_copy(1, 0, slot, me(z=zs)).wait_recv()
    vg_copies[2].start()
    axo[0].wait_recv()
    ay[3].start()
    axo[2].wait_recv()
    ay[1].start()
    token_sends(2)
    axi[0].start()
    axi[2].start()

    pl.semaphore_wait(near_sem, 2)
    tell(two_sem, 2)
    for sl in (1, 2 + c):
        vg_copy(0, 0, sl, me(c=1 - c)).wait_recv()
    for sl in (1, 2, 3):
        send(invs.at[0], invs.at[sl], inv_s.at[0], inv_r.at[sl - 1], me(c=1 - c)).wait_recv()
    for sl in range(4):
        scale = jnp.concatenate([invs[sl]] * 16, axis=0).T[:, 0:1]
        rows = pl.ds(sl * T, T)
        vgall[rows] = (vgraw[rows].astype(F32) * scale).astype(BF)

    def a1_copy(ht):
        return send(
            s1.at[(x + 2) % NX, pl.ds(ht * 2, 2)], a1.at[ht], a1_s.at[ht], a1_r.at[ht], me(x=(x + (1, 3)[ht]) % NX)
        )

    def a2_copy(m):
        xt = (x + STEPS[m]) % NX
        return send(s2.at[(y + 2) % NY, xt], a2.at[m], a2_s.at[m], a2_r.at[m], me(y=(y + (1, 3)[m % 2]) % NY))

    def p1_copy(d, ht):
        return send(
            s1.at[(x + d) % NX, pl.ds(ht * 2, 2)], r1.at[d // 2, pl.ds(ht * 2, 2)],
            p1_s.at[d // 2, ht], p1_r.at[d // 2, ht], me(x=(x + d) % NX),
        )

    def p2_copy(e, m):
        xt = (x + STEPS[m]) % NX
        return send(
            s2.at[(y + e) % NY, xt], r2.at[e // 2, xt], p2_s.at[e // 2, m], p2_r.at[e // 2, m], me(y=(y + e) % NY)
        )

    def weight_tile(xt, ht):
        total = lax.dot_general(nall[xt, ht], vgall[...], (((0,), (0,)), ((), ())), preferred_element_type=F32)
        total = total.astype(BF).reshape(8, 2, 16, K)
        for low in range(2):
            part = total[:, low].reshape(128, K)
            s1[xt, ht * 2 + low] = part[:, 0:256]
            s2[ht * 2 + low, xt] = part[:, 256:512]

    def weight_step(m):
        d = STEPS[m]
        xt = (x + d) % NX
        for ht in range(2):
            for sl in (1, 2, 3):
                send(
                    nall.at[xt, ht, pl.ds(0, T)], nall.at[xt, ht, pl.ds(sl * T, T)],
                    tok_s.at[0, xt, ht], tok_r.at[sl - 1, xt, ht], me(c=1 - c),
                ).wait_recv()
            weight_tile(xt, ht)
            if d == 2:
                a1_copy(ht).start()
            elif d != 0:
                if (d, ht) in ((1, 0), (3, 1)):
                    a1_copy(ht).wait_recv()
                    rows = pl.ds(ht * 2, 2)
                    s1[xt, rows] = (s1[xt, rows].astype(F32) + a1[ht].astype(F32)).astype(BF)
                p1_copy(d, ht).start()
        a2_copy(m).start()
        p2_copy((3, 1)[m % 2], m).start()

    def relay(m):
        e, xt = (1, 3)[m % 2], (x + STEPS[m]) % NX
        yt = (y + e) % NY
        a2_copy(m).wait_recv()
        s2[yt, xt] = (s2[yt, xt].astype(F32) + a2[m].astype(F32)).astype(BF)
        p2_copy(e, m).start()

    owners = [(me(c=1 - c), 1), (me(z=zup, c=1), 3 - c), (me(z=zdn, c=0), 2 + c)]

    def back_copy(i, xt, ht):
        to, j = owners[i]
        return send(
            ngs.at[xt, ht, pl.ds(i * T, T)], ngr.at[j, xt, ht], back_s.at[i, xt, ht], back_r.at[j - 1, xt, ht], to
        )

    def grad_tile(xt, ht):
        ng = lax.dot_general(
            vgall[...], wall[xt, ht], (((1,), (1,)), ((), ())), preferred_element_type=F32
        ).astype(BF)
        ngr[0, xt, ht] = ng[0:T]
        ngs[xt, ht] = ng[T:]
        for i in range(3):
            back_copy(i, xt, ht).start()

    weight_step(0)
    token_sends(3)
    pl.semaphore_wait(two_sem, 2)
    tell(four_sem, 4)
    axo[1].wait_recv()
    ay[2].start()
    axi[1].start()
    weight_step(1)
    ay_in[3].wait_recv()
    ap[3].start()
    weight_step(2)
    relay(0)
    ay_in[1].wait_recv()
    ap[1].start()
    weight_step(3)
    relay(1)
    ay_in[2].wait_recv()
    ap[2].start()
    for copy in axi:
        copy.wait_recv()

    def near_tile(i, carry):
        grad_tile((x + i) % NX, yh)
        return carry

    lax.fori_loop(0, NX, near_tile, 0)
    ay_in[0].wait_recv()
    grad_tile(x, 1 - yh)

    def q1_copy(e):
        return send(t1.at[(y + e) % NY], u1.at[e - 1], q1_s.at[e - 1], q1_r.at[e - 1], me(y=(y + e) % NY))

    def q2_copy(d):
        return send(t2.at[(x + d) % NX], u2.at[d - 1], q2_s.at[d - 1], q2_r.at[d - 1], me(x=(x + d) % NX))

    for m in (2, 3):
        relay(m)
    for ht in range(2):
        for d in (1, 3):
            p1_copy(d, ht).wait_recv()

    def add1(e, carry):
        yt = (y + e) % NY
        total = s1[x, yt].astype(F32) + r1[0, yt].astype(F32) + r1[1, yt].astype(F32)
        t1[yt] = total.astype(BF)

        @pl.when(e != NY)
        def _():
            q1_copy(e).start()

        return carry

    lax.fori_loop(1, NY + 1, add1, 0)
    for m in range(NX):
        for e in (1, 3):
            p2_copy(e, m).wait_recv()

    def add2(d, carry):
        xt = (x + d) % NX
        total = s2[y, xt].astype(F32) + r2[0, xt].astype(F32) + r2[1, xt].astype(F32)
        t2[xt] = total.astype(BF)

        @pl.when(d != NX)
        def _():
            q2_copy(d).start()

        return carry

    lax.fori_loop(1, NX + 1, add2, 0)

    for d in (3, 1, 2):
        send(
            wall.at[(x + d) % NX, 1 - yh, out_half], wall.at[(x + d) % NX, 1 - yh, out_half],
            ap_s.at[d], ap_r.at[d], me(y=yh * 2 + 1 - yl),
        ).wait_recv()
        grad_tile((x + d) % NX, 1 - yh)

    for e in (1, 2, 3):
        q1_copy(e).wait_recv()
    total = t1[y].astype(F32) + u1[0].astype(F32) + u1[1].astype(F32) + u1[2].astype(F32)
    vb[:, :, 0:256] = total.astype(BF).reshape(8, 16, 256)
    for d in (1, 2, 3):
        q2_copy(d).wait_recv()
    total = t2[x].astype(F32) + u2[0].astype(F32) + u2[1].astype(F32) + u2[2].astype(F32)
    vb[:, :, 256:512] = total.astype(BF).reshape(8, 16, 256)

    pl.semaphore_wait(four_sem, 2)

    def z_copy(k):
        return send(vb.at[k], zr.at[z // 2], z_s.at[k], z_r.at[z // 2], me(z=p * 8 + k))

    def z_start(i, carry):
        k = (z + i) % 8

        @pl.when(p * 8 + k != z)
        def _():
            z_copy(k).start()

        @pl.when(p * 8 + k == z)
        def _():
            zr[z // 2] = vb[k]

        return carry

    lax.fori_loop(0, 8, z_start, 0)

    def returned(ht):
        for j in (1, 2, 3):
            for xt in range(NX):
                send(
                    ngs.at[xt, ht, pl.ds(0, T)], ngr.at[j, xt, ht],
                    back_s.at[0, xt, ht], back_r.at[j - 1, xt, ht], me(c=1 - c),
                ).wait_recv()

    def feature_tile(j, xt, ht):
        return ngr[j, xt, ht].astype(F32) * gain_ref[:, pl.ds(column(j, xt, ht), F)]

    def token_tile(j, xt, ht):
        return tok[:, pl.ds(column(j, xt, ht), F)].astype(F32)

    def add_spread(ht, acc):
        def spread_tile(xt, acc):
            for j in range(4):
                prod = feature_tile(j, xt, ht) * token_tile(j, xt, ht)
                acc = acc + (prod[:, 0:128] + prod[:, 128:256])
            return acc

        return lax.fori_loop(0, NX, spread_tile, acc)

    returned(yh)
    acc = add_spread(yh, jnp.zeros((T, 128), F32))
    returned(1 - yh)
    acc = add_spread(1 - yh, acc)
    spread = jnp.sum(acc, axis=1, keepdims=True) * (1.0 / D) * (inv_rms * inv_rms)

    def input_tile(i, carry):
        xt, ht = i // 2, i % 2
        for j in range(4):
            grad = feature_tile(j, xt, ht) - token_tile(j, xt, ht) * spread
            ig_ref[:, pl.ds(column(j, xt, ht), F)] = grad.astype(BF)
        return carry

    lax.fori_loop(0, 8, input_tile, 0)

    def z_wait(k, carry):
        @pl.when(2 * k + z // 8 != z)
        def _():
            send(vb.at[k], zr.at[k], z_s.at[k], z_r.at[k], me(z=(z + 1) % NZ)).wait_recv()

        return carry

    lax.fori_loop(0, 8, z_wait, 0)
    total = zr[0].astype(F32)
    for k in range(1, 8):
        total = total + zr[k].astype(F32)

    lanes = lax.broadcasted_iota(jnp.int32, (16, 128), 1)
    rows = lax.broadcasted_iota(jnp.int32, (16, 128), 0)
    block = gain_ref[:, pl.ds(pl.multiple_of(node * 512 + (dp // 8) * 128, 128), 128)]
    picked = jnp.where(lanes == rows + (dp % 8) * 16, jnp.broadcast_to(block, (16, 128)), 0.0)
    wg_ref[...] = total * jnp.sum(picked, axis=1, keepdims=True)
    own = shard[pl.ds(pl.multiple_of(dp * 16, 16), 16)].astype(F32)
    gain_sum = jnp.sum(own * total, axis=1, keepdims=True)
    spread_out = jnp.where(lanes == rows, jnp.broadcast_to(gain_sum, (16, 128)), 0.0)
    gg_ref[...] = jnp.sum(spread_out, axis=0, keepdims=True)

    for copy in vg_copies + axo + axi + ay + [ap[1], ap[2], ap[3]]:
        copy.wait_send()
    for i in range(3):
        inv_copy(i).wait_send()
        for xt in range(NX):
            for ht in range(2):
                token_copy(i, xt, ht).wait_send()
                back_copy(i, xt, ht).wait_send()
        q1_copy(i + 1).wait_send()
        q2_copy(i + 1).wait_send()

    for ht in range(2):
        a1_copy(ht).wait_send()
        for d in (1, 3):
            p1_copy(d, ht).wait_send()
    for m in range(NX):
        a2_copy(m).wait_send()
        for e in (1, 3):
            p2_copy(e, m).wait_send()

    def z_sent(k, carry):
        @pl.when(p * 8 + k != z)
        def _():
            z_copy(k).wait_send()

        return carry

    lax.fori_loop(0, 8, z_sent, 0)


def on_device(tokens_in, gain, value_weight, value_grad):
    vmem, dma = pltpu.VMEM, pltpu.SemaphoreType.DMA
    scratch = [
        vmem((T, D), BF), vmem((1, D), F32), vmem((K, K), BF), vmem((4 * T, K), BF), vmem((4 * T, K), BF), vmem((4, 8, 128), F32),
        vmem((NX, 2, 4 * T, F), BF), vmem((NX, 2, F, K), BF),
        vmem((NX, 2, 3 * T, F), BF), vmem((4, NX, 2, T, F), BF),
        vmem((NX, NY, 128, 256), BF), vmem((NY, NX, 128, 256), BF),
        vmem((2, 2, 128, 256), BF), vmem((NX, 128, 256), BF),
        vmem((2, NY, 128, 256), BF), vmem((2, NX, 128, 256), BF),
        vmem((NY, 128, 256), BF), vmem((NX, 128, 256), BF),
        vmem((3, 128, 256), BF), vmem((3, 128, 256), BF),
        vmem((8, 16, K), BF), vmem((8, 16, K), BF),
    ]
    sems = [(4,)] + [(3,)] * 4 + [(3, NX, 2)] * 2 + [(2, 3)] * 2 + [(4,)] * 4 + [(3, NX, 2)] * 2
    sems += [(2,)] * 2 + [(NX,)] * 2 + [(2, 2)] * 2 + [(2, NX)] * 2 + [(3,)] * 4 + [(8,)] * 2
    operands = (tokens_in, gain.reshape(1, D), value_weight, value_grad)
    operands = [pltpu.with_memory_space_constraint(a, pltpu.HBM) for a in operands]
    in_hbm = pl.BlockSpec(memory_space=pltpu.HBM)
    in_vmem = pl.BlockSpec(memory_space=pltpu.VMEM)
    weight_grad, gain_grad, input_grad = pl.pallas_call(
        kernel,
        out_shape=(
            jax.ShapeDtypeStruct((16, K), F32),
            jax.ShapeDtypeStruct((1, 128), F32),
            jax.ShapeDtypeStruct((T, D), BF),
        ),
        in_specs=[in_hbm] * 4,
        out_specs=(in_vmem, in_vmem, in_vmem),
        scratch_shapes=scratch + [dma(s) for s in sems] + [pltpu.SemaphoreType.REGULAR] * 3,
        compiler_params=pltpu.CompilerParams(
            collective_id=0, has_side_effects=True, vmem_limit_bytes=40 * 1024 * 1024
        ),
    )(*operands)
    return weight_grad, gain_grad[0, :16], input_grad


def solution(mesh):
    placed = (P(("node", "dp"), None), P(), P("node", None), P(("node", "dp"), None))
    return jax.shard_map(
        on_device,
        mesh=mesh,
        in_specs=placed,
        out_specs=(P(("node", "dp"), None), P(("node", "dp")), P(("node", "dp"), None)),
        check_vma=False,
    )
```
